32 devices in a mesh: grp: 4 (over y, x), dev: 8 (over z, core).
Axes of the slice: x: 2, y: 2, z: 4, core: 2. Of those that a mesh axis runs over, the one named last changes fastest.
Arguments:
- image_tokens: bfloat16 [128, 197, 768], P(('grp', 'dev')), may hold values from -64 to 64
- text_tokens: bfloat16 [128, 30, 768], P(('grp', 'dev')), may hold values from -64 to 64
- negatives: int32 [128, 2], P(('grp', 'dev')), may hold values from 0 to 31, as said below
- query_weight: bfloat16 [768, 768], replicated, may hold values from -0.21875 to 0.21875
- kv_weight: bfloat16 [768, 1536], replicated, may hold values from -0.21875 to 0.21875
- match_head: float32 [768], replicated, may hold values from -6 to 6
- cotangent: bfloat16 [128, 3], P(('grp', 'dev')), may hold values from -6 to 6
Outputs:
- logits: float32 [128, 3], P(('grp', 'dev'))
- grad_query_weight: float32 [768, 768], P(('grp', 'dev'))
- grad_kv_weight: float32 [768, 1536], P(('grp', 'dev'))
The draws below stay inside these ranges and needn't reach their ends.
Inputs may be any that keep to these rules, and one draw needn't show every extreme that they name: At most 2 of the 8 negatives of one device lie on any one device of its group, and in every group some device holds exactly 2 negatives of every device of the group.
All inputs are finite; a program needn't handle non-finite values.
Results may differ from the reference program's by a relative error of at most 0.0085.
The reference program's roundings to bfloat16 on the way count: a program that leaves them out, or rounds other values in their place, can miss the bound.
Values may be sent and summed in bfloat16 or wider, within the bound.
A program may use at most 128 MiB of HBM per device.

```python
import jax
import jax.numpy as jnp
from jax import lax

D = 768
HEADS = 12
LI = 197
LT = 30
PAIR_DEV = 4
TEXTS = 128
N_GRP = 4
N_DEV = 8


def token_rows(key, count, length):
    shape = (count, length, D)
    values = jnp.clip(jax.random.normal(jax.random.fold_in(key, 5), shape, jnp.float32), -6.0, 6.0)
    return values


def draw_image_tokens(key, part):
    return token_rows(jax.random.fold_in(key, 101), PAIR_DEV * N_GRP * N_DEV, LI).astype(jnp.bfloat16)


def draw_text_tokens(key, part):
    return token_rows(jax.random.fold_in(key, 202), PAIR_DEV * N_GRP * N_DEV, LT).astype(jnp.bfloat16)


def draw_negatives(key, part):
    capacity = max(2, (2 * PAIR_DEV + N_DEV - 1) // N_DEV)
    requests = 2 * PAIR_DEV

    def one_block(block_key, popular):
        others = (popular + 1 + jnp.tile(jnp.arange(N_DEV - 1, dtype=jnp.int32), capacity)) % N_DEV
        spread = jax.random.permutation(jax.random.fold_in(block_key, 1), others)[:requests - capacity]
        owners = jnp.concatenate([jnp.full((capacity,), popular, jnp.int32), spread])
        owners = jax.random.permutation(jax.random.fold_in(block_key, 2), owners)
        inner = jax.random.randint(jax.random.fold_in(block_key, 3), (requests,), 0, PAIR_DEV, dtype=jnp.int32)
        return (owners * PAIR_DEV + inner).reshape(PAIR_DEV, 2)
    popular_owner = jax.random.randint(jax.random.fold_in(key, 7), (N_GRP,), 0, N_DEV, dtype=jnp.int32)
    block_keys = jax.random.split(jax.random.fold_in(key, 11), N_GRP * N_DEV)
    populars = jnp.repeat(popular_owner, N_DEV)
    blocks = jax.vmap(one_block)(block_keys, populars)
    return blocks.reshape(-1, 2)


def shard_levels(own_key, extent, cuts, low, top_value):
    def one(dim, blocks):
        steps = jax.random.uniform(jax.random.fold_in(jax.random.fold_in(own_key, 6), dim), (blocks,), jnp.float32, low / len(cuts), top_value / len(cuts))
        return jnp.repeat(jnp.exp(steps), extent[dim] // blocks).reshape((-1,) + (1,) * (len(extent) - dim - 1))

    factor_of = one(*cuts[0])
    for cut in cuts[1:]:
        factor_of = factor_of * one(*cut)
    return factor_of


def scatter_about(stream_key, dims, deviation, most, pieces=(), kind=jnp.bfloat16):
    values = jax.random.normal(stream_key, dims, jnp.float32) * deviation
    if len(pieces) > 0:
        values = shard_levels(stream_key, dims, pieces, -0.22, 0.18) * values
    return jnp.clip(values, min=-most, max=most).astype(kind)


def setup_inputs(seed: int = 0) -> dict:
    streams_of = jax.random.split(jax.random.key(seed), 8)
    image_tokens = draw_image_tokens(jax.random.fold_in(streams_of[7], 71), 0)
    text_tokens = draw_text_tokens(jax.random.fold_in(streams_of[7], 71), 0)
    negatives = draw_negatives(jax.random.fold_in(streams_of[7], 71), 0)
    query_weight = scatter_about(streams_of[3], (D, D), D ** -0.5, 0.21875)
    kv_weight = scatter_about(streams_of[4], (D, 2 * D), D ** -0.5, 0.21875)
    match_head = scatter_about(streams_of[5], (D,), 1.0, 6.0, (), jnp.float32)
    cotangent = scatter_about(streams_of[6], (TEXTS, 3), 1.0, 6.0, ((0, 32),))
    return {"image_tokens": image_tokens, "text_tokens": text_tokens, "negatives": negatives, "query_weight": query_weight, "kv_weight": kv_weight, "match_head": match_head, "cotangent": cotangent}


def attend(queries, keys_values, tangent, match_head):
    count = queries.shape[0]
    text_len = queries.shape[1]
    image_len = keys_values.shape[1]
    model = queries.shape[2]
    head_size = model // HEADS
    factor = head_size ** -0.5
    query_heads = queries.astype(jnp.float32).reshape(count, text_len, HEADS, head_size)
    key_heads = keys_values[..., :model].astype(jnp.float32).reshape(count, image_len, HEADS, head_size)
    value_heads = keys_values[..., model:].astype(jnp.float32).reshape(count, image_len, HEADS, head_size)
    scores = jnp.einsum("bqhd,bkhd->bhqk", query_heads, key_heads, precision=lax.Precision.HIGHEST) * factor
    probs = jax.nn.softmax(scores, axis=-1)
    probs_low = probs.astype(jnp.bfloat16).astype(jnp.float32)
    context = jnp.einsum("bhqk,bkhd->bqhd", probs_low, value_heads, precision=lax.Precision.HIGHEST)
    pooled = jnp.mean(context, axis=1).reshape(count, model)
    logits = jnp.sum(pooled * match_head[None, :], axis=-1)
    direction = (tangent / text_len)[:, None] * match_head[None, :]
    dir_heads = direction.reshape(count, HEADS, head_size)
    d_probs = jnp.einsum("bkhd,bhd->bhk", value_heads, dir_heads, precision=lax.Precision.HIGHEST)
    d_scores = probs * (d_probs[:, :, None, :] - jnp.sum(probs * d_probs[:, :, None, :], axis=-1, keepdims=True))
    d_low = d_scores.astype(jnp.bfloat16).astype(jnp.float32)
    d_keys = jnp.einsum("bhqk,bqhd->bkhd", d_low, query_heads, precision=lax.Precision.HIGHEST) * factor
    d_queries = jnp.einsum("bhqk,bkhd->bqhd", d_low, key_heads, precision=lax.Precision.HIGHEST) * factor
    weight_sum = jnp.sum(probs_low, axis=2)
    d_values = jnp.transpose(weight_sum[..., None] * dir_heads[:, :, None, :], (0, 2, 1, 3))
    kv_grad = jnp.concatenate([d_keys.reshape(count, image_len, model), d_values.reshape(count, image_len, model)], axis=-1)
    return logits, kv_grad, d_queries.reshape(count, text_len, model)


def reference(image_tokens, text_tokens, negatives, query_weight, kv_weight, match_head, cotangent):
    text_count = text_tokens.shape[0]
    group_size = PAIR_DEV * N_DEV
    queries = jnp.dot(text_tokens.reshape(-1, D), query_weight, preferred_element_type=jnp.float32).astype(jnp.bfloat16).reshape(text_count, LT, D)
    keys_values = jnp.dot(image_tokens.reshape(-1, D), kv_weight, preferred_element_type=jnp.float32).astype(jnp.bfloat16).reshape(-1, LI, 2 * D)
    position = jnp.arange(text_count, dtype=jnp.int32)
    offset = (position // group_size) * group_size
    chosen = jnp.concatenate([position[:, None], offset[:, None] + negatives.astype(jnp.int32)], axis=1)

    def one_text(carry, item):
        grad_query, grad_kv = carry
        picks, text_query, text_rows, tangent = item
        pictures = image_tokens[picks]
        chosen_kv = keys_values[picks]
        repeated = jnp.broadcast_to(text_query[None], (3, LT, D))
        logit_row, kv_grad, query_grad = attend(repeated, chosen_kv, tangent.astype(jnp.float32), match_head)
        kv_low = kv_grad.astype(jnp.bfloat16).reshape(-1, 2 * D)
        grad_kv = grad_kv + jnp.dot(pictures.reshape(-1, D).T, kv_low, preferred_element_type=jnp.float32)
        total_query = jnp.sum(query_grad, axis=0).astype(jnp.bfloat16)
        grad_query = grad_query + jnp.dot(text_rows.T, total_query, preferred_element_type=jnp.float32)
        return (grad_query, grad_kv), logit_row

    start = (jnp.zeros((D, D), jnp.float32), jnp.zeros((D, 2 * D), jnp.float32))
    (grad_query_weight, grad_kv_weight), logits = lax.scan(one_text, start, (chosen, queries, text_tokens, cotangent))
    return logits, grad_query_weight, grad_kv_weight
```

```python
import functools

import jax
import jax.numpy as jnp
import numpy as np
from jax import lax
from jax.experimental import pallas as pl
from jax.experimental.pallas import tpu as pltpu
from jax.sharding import PartitionSpec as P

HEADS = 12
PACK = 4
ROWS = 32
BF = jnp.bfloat16
F32 = jnp.float32
VMEM = pl.BlockSpec(memory_space=pltpu.VMEM)
SMEM = pl.BlockSpec(memory_space=pltpu.SMEM)
BIG = 56 * 1024 * 1024


def up(value, unit):
    return (value + unit - 1) // unit * unit


def nt(left, right):
    return lax.dot_general(left, right, (((1,), (1,)), ((), ())), preferred_element_type=F32)


def tn(left, right):
    return lax.dot_general(left, right, (((0,), (0,)), ((), ())), preferred_element_type=F32)


def nn(left, right):
    return jnp.dot(left, right, preferred_element_type=F32)


def keys_kernel(x_ref, w_ref, mh_ref, k_ref, u_ref, xp_ref):
    count, length, model = x_ref.shape
    head = model // HEADS
    gain = mh_ref[...]
    high = gain.astype(BF).astype(F32)
    middle = (gain - high).astype(BF).astype(F32)
    low = gain - high - middle
    rows = lax.broadcasted_iota(jnp.int32, (16, model), 0)
    lanes = lax.broadcasted_iota(jnp.int32, (16, model), 1)
    inside = (lanes >= rows * head) & (lanes < rows * head + head)
    parts = [jnp.where(inside, part, 0.0).astype(BF) for part in (high, middle, low)]
    for image in range(count):
        xp_ref[image] = jnp.zeros(xp_ref.shape[1:], BF)
        xp_ref[image, :length, :] = x_ref[image]
        rows_in = xp_ref[image]
        k_ref[image] = nn(rows_in, w_ref[:, :model]).astype(BF)
        values = nn(rows_in, w_ref[:, model:]).astype(BF)
        u_ref[image] = nt(parts[0], values) + nt(parts[1], values) + nt(parts[2], values)


def pairs_kernel(
    length, text_len, owner_ref, local_ref, tangent_ref, feat_k_ref, feat_q_ref, x_ref, k_ref,
    u_ref, t_ref, wq_ref, gk_ref, gq_ref, at_ref, lg_ref,
    tp_ref, q_ref, dk_ref, dq_ref, s_ref, text_s, col_s, image_s,
):
    count, padded, model = k_ref.shape
    head = model // HEADS
    width = PACK * head
    block = PACK * ROWS
    factor = head ** (-0.5)
    me = lax.axis_index("dev")
    requests = owner_ref.shape[0]
    real = lax.broadcasted_iota(jnp.int32, (ROWS, model), 0) < text_len

    def place(slot, text):
        rows = jnp.where(real, t_ref[text].astype(F32), 0.0).astype(BF)
        tp_ref[pl.ds(pl.multiple_of(slot * ROWS, ROWS), ROWS), :] = rows

    tp_ref[...] = jnp.zeros(tp_ref.shape, BF)
    dq_ref[...] = jnp.zeros(dq_ref.shape, BF)
    dk_ref[...] = jnp.zeros(dk_ref.shape, F32)
    s_ref[...] = jnp.zeros(s_ref.shape, F32)
    lg_ref[...] = jnp.zeros(lg_ref.shape, F32)
    for image in range(count):
        text_s[image] = me * count + image
        col_s[image] = 0
        image_s[image] = image
        place(image, me * count + image)

    def look(request, filled):
        mine = owner_ref[request] == me

        @pl.when(mine)
        def _():
            text = request // 2
            text_s[filled] = text
            col_s[filled] = request - 2 * text + 1
            image_s[filled] = local_ref[request]
            place(filled, text)

        return filled + mine.astype(jnp.int32)

    used = lax.fori_loop(0, requests, look, jnp.int32(count))
    q_ref[...] = nn(tp_ref[...], wq_ref[...]).astype(BF)

    row_head = lax.broadcasted_iota(jnp.int32, (block, width), 0) // ROWS
    lane_head = lax.broadcasted_iota(jnp.int32, (block, width), 1) // head
    diagonal = row_head == lane_head
    short_head = lax.broadcasted_iota(jnp.int32, (ROWS, width), 1) // head
    beyond = lax.broadcasted_iota(jnp.int32, (block, padded), 1) >= length
    sum_row = lax.broadcasted_iota(jnp.int32, (16, block), 0)
    sum_lane = lax.broadcasted_iota(jnp.int32, (16, block), 1)
    counted = (sum_lane // ROWS == sum_row) & (sum_lane % ROWS < text_len)
    summer = jnp.where(counted, 1.0, 0.0).astype(BF)

    def pair(slot, carry):
        image = image_s[slot]
        where = text_s[slot] * 3 + col_s[slot]
        scale = tangent_ref[where] / text_len
        rows = pl.ds(pl.multiple_of(slot * ROWS, ROWS), ROWS)
        total = jnp.zeros((1, padded), F32)
        for pack in range(HEADS // PACK):
            cols = slice(pack * width, (pack + 1) * width)
            four = q_ref[rows, cols].astype(F32)
            tall = jnp.concatenate([four] * PACK, axis=0)
            spread = jnp.where(diagonal, tall, 0.0).astype(BF)
            keys = k_ref[image, :, cols]
            scores = nt(spread, keys) * factor
            scores = jnp.where(beyond, -1e30, scores)
            scores = jnp.exp(scores - jnp.max(scores, axis=1, keepdims=True))
            probs = scores * (1.0 / jnp.sum(scores, axis=1, keepdims=True))
            weight_sum = nn(summer, probs.astype(BF))[:PACK]
            gains = u_ref[image, pack * PACK:(pack + 1) * PACK, :]
            total = total + jnp.sum(weight_sum * gains, axis=0, keepdims=True)
            s_ref[image, pack * PACK:(pack + 1) * PACK, :] += weight_sum * scale
            d_probs = jnp.concatenate(
                [jnp.broadcast_to(gains[h:h + 1], (ROWS, padded)) for h in range(PACK)], axis=0
            ) * scale
            centre = jnp.sum(probs * d_probs, axis=1, keepdims=True)
            d_low = (probs * (d_probs - centre)).astype(BF)
            dk_ref[image, :, cols] += tn(d_low, spread)
            wide = nn(d_low, keys)
            kept = jnp.zeros((ROWS, width), F32)
            for h in range(PACK):
                kept = jnp.where(short_head == h, wide[h * ROWS:(h + 1) * ROWS], kept)
            dq_ref[rows, cols] = (kept * factor).astype(BF)
        lg_ref[pl.ds(where, 1), :] = total * (1.0 / text_len)
        return carry

    lax.fori_loop(0, used, pair, 0)

    def one_hot(feat):
        lanes = lax.broadcasted_iota(jnp.int32, (feat.shape[0], model), 1)
        return jnp.where(lanes == feat, 1.0, 0.0).astype(BF)

    turn_q = one_hot(feat_q_ref[...])
    gq_ref[...] = nn(nt(turn_q, tp_ref[...]).astype(BF), dq_ref[...]).astype(gq_ref.dtype)
    turn_k = one_hot(feat_k_ref[...])
    for image in range(count):
        x_ref_rows = x_ref[image]
        flipped = nt(turn_k, x_ref_rows).astype(BF)
        part = nn(flipped, (dk_ref[image] * factor).astype(BF))
        weights = s_ref[image]
        high = weights.astype(BF)
        low = (weights - high.astype(F32)).astype(BF)
        sums = nn(high, x_ref_rows) + nn(low, x_ref_rows)
        if image == 0:
            gk_ref[...] = part
            at_ref[...] = sums
        else:
            gk_ref[...] += part
            at_ref[...] += sums


def feature_rows(model, total):
    return np.arange(model, dtype=np.int32)[:, None]


def local(image_tokens, text_tokens, negatives, query_weight, kv_weight, match_head, cotangent):
    count, length, model = image_tokens.shape
    text_len = text_tokens.shape[1]
    devices = lax.axis_size("dev")
    groups = lax.axis_size("grp")
    capacity = max(2, (2 * count + devices - 1) // devices)
    padded = up(length, 256)
    texts = devices * count
    slots = count + devices * capacity

    owner = negatives // count
    meta = jnp.concatenate(
        [cotangent, owner.astype(BF), (negatives - owner * count).astype(BF)], axis=1
    )
    meta = jnp.pad(meta, ((0, 0), (0, model - meta.shape[1])))[:, None, :]
    message = jnp.concatenate(
        [text_tokens, meta, jnp.zeros((count, ROWS - text_len - 1, model), BF)], axis=1
    )
    everyone = lax.all_gather(message, "dev", axis=0, tiled=True)

    keys, gains, pictures = pl.pallas_call(
        keys_kernel,
        out_shape=(
            jax.ShapeDtypeStruct((count, padded, model), BF),
            jax.ShapeDtypeStruct((count, 16, padded), F32),
            jax.ShapeDtypeStruct((count, padded, model), BF),
        ),
        in_specs=[VMEM] * 3,
        out_specs=(VMEM,) * 3,
        compiler_params=pltpu.CompilerParams(vmem_limit_bytes=BIG),
        cost_estimate=pl.CostEstimate(
            flops=4 * count * padded * model * model, bytes_accessed=8 * 1024 * 1024,
            transcendentals=0,
        ),
    )(image_tokens, kv_weight, match_head.reshape(1, model))

    facts = everyone[:, text_len, :8].astype(F32)
    owners = facts[:, 3:5].astype(jnp.int32).reshape(-1)
    locals_ = facts[:, 5:7].astype(jnp.int32).reshape(-1)
    tangents = facts[:, :3].reshape(-1)
    feat = feature_rows(model, groups * devices)
    span = feat.shape[0]
    grad_k, grad_q, sums, parts = pl.pallas_call(
        functools.partial(pairs_kernel, length, text_len),
        out_shape=(
            jax.ShapeDtypeStruct((span, model), F32),
            jax.ShapeDtypeStruct((span, model), BF),
            jax.ShapeDtypeStruct((16, model), F32),
            jax.ShapeDtypeStruct((texts * 3, padded), F32),
        ),
        in_specs=[SMEM] * 3 + [VMEM] * 7,
        out_specs=(VMEM,) * 4,
        scratch_shapes=[
            pltpu.VMEM((slots * ROWS, model), BF),
            pltpu.VMEM((slots * ROWS, model), BF),
            pltpu.VMEM((count, padded, model), F32),
            pltpu.VMEM((slots * ROWS, model), BF),
            pltpu.VMEM((count, 16, padded), F32),
            pltpu.SMEM((slots,), jnp.int32),
            pltpu.SMEM((slots,), jnp.int32),
            pltpu.SMEM((slots,), jnp.int32),
        ],
        compiler_params=pltpu.CompilerParams(vmem_limit_bytes=BIG),
        cost_estimate=pl.CostEstimate(
            flops=20 * 1024**3, bytes_accessed=16 * 1024 * 1024, transcendentals=0
        ),
    )(owners, locals_, tangents, feat, feat, pictures, keys, gains, everyone, query_weight)

    both = jnp.stack([grad_q, grad_k.astype(BF)], axis=1).reshape(span, 2 * model)
    grads = lax.psum_scatter(both, ("grp", "dev"), scatter_dimension=0, tiled=True).astype(F32)
    rows = model // (groups * devices)
    answers = jnp.sum(parts, axis=1).reshape(devices, count * 3)
    answers = jnp.where(
        jnp.arange(groups)[:, None, None] == lax.axis_index("grp"), answers[None], 0.0
    ).reshape(groups * devices, count * 3)
    factors = sums[:HEADS].T.reshape(groups * devices, rows * HEADS)
    small = lax.psum_scatter(
        jnp.concatenate([factors, answers], axis=1), ("grp", "dev"), scatter_dimension=0, tiled=True
    )
    logits = small[0, rows * HEADS:].reshape(count, 3)
    value_part = jnp.repeat(
        small[0, :rows * HEADS].reshape(rows, HEADS), model // HEADS, axis=1
    ) * match_head[None, :]
    return (
        logits, grads[:, :model], jnp.concatenate([grads[:, model:], value_part], axis=1)
    )


def solution(mesh):
    placed = (
        P(("grp", "dev"), None, None),
        P(("grp", "dev"), None, None),
        P(("grp", "dev"), None),
        P(),
        P(),
        P(),
        P(("grp", "dev"), None),
    )
    return jax.shard_map(
        local,
        mesh=mesh,
        in_specs=placed,
        out_specs=(P(("grp", "dev"), None), P(("grp", "dev"), None), P(("grp", "dev"), None)),
        check_vma=False,
    )
```

```python
import functools

import jax
import jax.numpy as jnp
import numpy as np
from jax import lax
from jax.experimental import pallas as pl
from jax.experimental.pallas import tpu as pltpu
from jax.sharding import PartitionSpec as P

HEADS = 12
PACK = 4
ROWS = 32
BF = jnp.bfloat16
F32 = jnp.float32
VMEM = pl.BlockSpec(memory_space=pltpu.VMEM)
SMEM = pl.BlockSpec(memory_space=pltpu.SMEM)
BIG = 56 * 1024 * 1024


def up(value, unit):
    return (value + unit - 1) // unit * unit


def nt(left, right):
    return lax.dot_general(left, right, (((1,), (1,)), ((), ())), preferred_element_type=F32)


def tn(left, right):
    return lax.dot_general(left, right, (((0,), (0,)), ((), ())), preferred_element_type=F32)


def nn(left, right):
    return jnp.dot(left, right, preferred_element_type=F32)


def keys_kernel(x_ref, w_ref, mh_ref, k_ref, u_ref, xp_ref):
    count, length, model = x_ref.shape
    head = model // HEADS
    gain = mh_ref[...]
    high = gain.astype(BF).astype(F32)
    middle = (gain - high).astype(BF).astype(F32)
    low = gain - high - middle
    rows = lax.broadcasted_iota(jnp.int32, (16, model), 0)
    lanes = lax.broadcasted_iota(jnp.int32, (16, model), 1)
    inside = (lanes >= rows * head) & (lanes < rows * head + head)
    parts = [jnp.where(inside, part, 0.0).astype(BF) for part in (high, middle, low)]
    for image in range(count):
        xp_ref[image] = jnp.zeros(xp_ref.shape[1:], BF)
        xp_ref[image, :length, :] = x_ref[image]
        rows_in = xp_ref[image]
        k_ref[image] = nn(rows_in, w_ref[:, :model]).astype(BF)
        values = nn(rows_in, w_ref[:, model:]).astype(BF)
        u_ref[image] = nt(parts[0], values) + nt(parts[1], values) + nt(parts[2], values)


def pairs_kernel(
    length, text_len, owner_ref, local_ref, tangent_ref, feat_k_ref, feat_q_ref, home_ref, x_ref,
    k_ref, u_ref, t_ref, wq_ref, gk_ref, gq_ref, small_ref,
    tp_ref, q_ref, dk_ref, dq_ref, s_ref, lg_ref, text_s, col_s, image_s,
):
    count, padded, model = k_ref.shape
    head = model // HEADS
    width = PACK * head
    block = PACK * ROWS
    factor = head ** (-0.5)
    me = lax.axis_index("dev")
    requests = owner_ref.shape[0]
    real = lax.broadcasted_iota(jnp.int32, (ROWS, model), 0) < text_len

    def place(slot, text):
        rows = jnp.where(real, t_ref[text].astype(F32), 0.0).astype(BF)
        tp_ref[pl.ds(pl.multiple_of(slot * ROWS, ROWS), ROWS), :] = rows

    tp_ref[...] = jnp.zeros(tp_ref.shape, BF)
    dq_ref[...] = jnp.zeros(dq_ref.shape, BF)
    dk_ref[...] = jnp.zeros(dk_ref.shape, F32)
    s_ref[...] = jnp.zeros(s_ref.shape, F32)
    lg_ref[...] = jnp.zeros(lg_ref.shape, F32)
    for image in range(count):
        text_s[image] = me * count + image
        col_s[image] = 0
        image_s[image] = image
        place(image, me * count + image)

    def look(request, filled):
        mine = owner_ref[request] == me

        @pl.when(mine)
        def _():
            text = request // 2
            text_s[filled] = text
            col_s[filled] = request - 2 * text + 1
            image_s[filled] = local_ref[request]
            place(filled, text)

        return filled + mine.astype(jnp.int32)

    used = lax.fori_loop(0, requests, look, jnp.int32(count))
    q_ref[...] = nn(tp_ref[...], wq_ref[...]).astype(BF)

    row_head = lax.broadcasted_iota(jnp.int32, (block, width), 0) // ROWS
    lane_head = lax.broadcasted_iota(jnp.int32, (block, width), 1) // head
    diagonal = row_head == lane_head
    short_head = lax.broadcasted_iota(jnp.int32, (ROWS, width), 1) // head
    beyond = lax.broadcasted_iota(jnp.int32, (block, padded), 1) >= length
    sum_row = lax.broadcasted_iota(jnp.int32, (16, block), 0)
    sum_lane = lax.broadcasted_iota(jnp.int32, (16, block), 1)
    counted = (sum_lane // ROWS == sum_row) & (sum_lane % ROWS < text_len)
    summer = jnp.where(counted, 1.0, 0.0).astype(BF)

    def pair(slot, carry):
        image = image_s[slot]
        where = text_s[slot] * 3 + col_s[slot]
        scale = tangent_ref[where] / text_len
        rows = pl.ds(pl.multiple_of(slot * ROWS, ROWS), ROWS)
        total = jnp.zeros((1, padded), F32)
        for pack in range(HEADS // PACK):
            cols = slice(pack * width, (pack + 1) * width)
            four = q_ref[rows, cols].astype(F32)
            tall = jnp.concatenate([four] * PACK, axis=0)
            spread = jnp.where(diagonal, tall, 0.0).astype(BF)
            keys = k_ref[image, :, cols]
            scores = nt(spread, keys) * factor
            scores = jnp.where(beyond, -1e30, scores)
            scores = jnp.exp(scores - jnp.max(scores, axis=1, keepdims=True))
            probs = scores * (1.0 / jnp.sum(scores, axis=1, keepdims=True))
            weight_sum = nn(summer, probs.astype(BF))[:PACK]
            gains = u_ref[image, pack * PACK:(pack + 1) * PACK, :]
            total = total + jnp.sum(weight_sum * gains, axis=0, keepdims=True)
            s_ref[image, pack * PACK:(pack + 1) * PACK, :] += weight_sum * scale
            d_probs = jnp.concatenate(
                [jnp.broadcast_to(gains[h:h + 1], (ROWS, padded)) for h in range(PACK)], axis=0
            ) * scale
            centre = jnp.sum(probs * d_probs, axis=1, keepdims=True)
            d_low = (probs * (d_probs - centre)).astype(BF)
            dk_ref[image, :, cols] += tn(d_low, spread)
            wide = nn(d_low, keys)
            kept = jnp.zeros((ROWS, width), F32)
            for h in range(PACK):
                kept = jnp.where(short_head == h, wide[h * ROWS:(h + 1) * ROWS], kept)
            dq_ref[rows, cols] = (kept * factor).astype(BF)
        lg_ref[pl.ds(where, 1), :] = total * (1.0 / text_len)
        return carry

    lax.fori_loop(0, used, pair, 0)

    def one_hot(feat):
        lanes = lax.broadcasted_iota(jnp.int32, (feat.shape[0], model), 1)
        return jnp.where(lanes == feat, 1.0, 0.0).astype(BF)

    blocks, tall_rows, half = gq_ref.shape
    lines = tall_rows // 2

    def store(out_ref, left, right):
        sides = [
            nn(left, right[:, side * half:(side + 1) * half]).reshape(blocks, lines, half)
            for side in range(2)
        ]
        out_ref[...] = jnp.concatenate(sides, axis=1).astype(BF)

    turn_q = one_hot(feat_q_ref[...])
    store(gq_ref, nt(turn_q, tp_ref[...]).astype(BF), dq_ref[...])
    turn_k = one_hot(feat_k_ref[...])
    pictures = x_ref[...].reshape(count * padded, model)
    flipped = nt(turn_k, pictures).astype(BF)
    store(gk_ref, flipped, (dk_ref[...] * factor).astype(BF).reshape(count * padded, model))

    answers = jnp.sum(lg_ref[...], axis=1, keepdims=True)
    outs = answers.shape[0]
    lane = lax.broadcasted_iota(jnp.int32, (outs, 128), 1)
    line = lax.broadcasted_iota(jnp.int32, (outs, 128), 0)
    rest = jnp.where(lane - 16 == line % (3 * count), answers, 0.0)
    homes = lax.broadcasted_iota(jnp.int32, (blocks * lines, outs), 0) == home_ref[...]
    homes = jnp.where(homes, 1.0, 0.0).astype(BF)
    small = jnp.zeros((blocks * lines, 128), F32)
    for step in range(3):
        piece = rest.astype(BF)
        rest = rest - piece.astype(F32)
        small = small + nn(homes, piece)
    for image in range(count):
        weights = s_ref[image]
        high = weights.astype(BF)
        low = (weights - high.astype(F32)).astype(BF)
        mine = flipped[:, image * padded:(image + 1) * padded]
        small = small + nt(mine, high) + nt(mine, low)
    small_ref[...] = small.reshape(blocks, lines, 128)


def reduce_kernel(
    rows, orders, k_ref, q_ref, small_ref, mh_ref, gq_ref, gkv_ref, logit_ref,
    k_acc, q_acc, s_acc, k_send, q_send, s_send, k_recv, q_recv, s_recv, send_sem, recv_sem,
):
    devices = lax.axis_size("dev")
    me = lax.axis_index("grp") * devices + lax.axis_index("dev")
    blocks = k_ref.shape[0]
    steps = len(orders[0])

    def bit_of(bit):
        return lax.rem(lax.div(me, 1 << bit), 2)

    def partner(bit):
        other = me + (1 - 2 * bit_of(bit)) * (1 << bit)
        return (lax.div(other, devices), lax.rem(other, devices))

    barrier = pltpu.get_barrier_semaphore()
    for bit in range(steps):
        pl.semaphore_signal(
            barrier, inc=1, device_id=partner(bit), device_id_type=pl.DeviceIdType.MESH
        )
    pl.semaphore_wait(barrier, steps)

    streams = (
        (k_ref, k_acc, k_send, k_recv, orders[0]),
        (q_ref, q_acc, q_send, q_recv, orders[1]),
        (small_ref, s_acc, s_send, s_recv, orders[0]),
    )
    copies = {}

    def send(index, step):
        source, acc, staged, landed, order = streams[index]
        size = blocks >> (step + 1)
        base = blocks - 2 * size
        away = (1 - bit_of(order[step])) * size
        if step == 0:
            held = source.at[pl.ds(away, size)]
        else:
            lower = base - blocks // 2
            held = staged.at[pl.ds(lower, size)]
            staged[pl.ds(lower, size)] = acc[pl.ds(start_of(order, step) + away, size)].astype(
                staged.dtype
            )
        copies[index, step] = pltpu.make_async_remote_copy(
            src_ref=held,
            dst_ref=landed.at[pl.ds(base, size)],
            send_sem=send_sem.at[index, step],
            recv_sem=recv_sem.at[index, step],
            device_id=partner(order[step]),
            device_id_type=pl.DeviceIdType.MESH,
        )
        copies[index, step].start()

    def start_of(order, step):
        start = 0
        for earlier in range(1, step):
            start = start + bit_of(order[earlier]) * (blocks >> (earlier + 1))
        return start

    def add(index, step):
        source, acc, staged, landed, order = streams[index]
        size = blocks >> (step + 1)
        base = blocks - 2 * size
        copies[index, step].wait_recv()
        arrived = landed[pl.ds(base, size)].astype(F32)
        keep = bit_of(order[step]) * size
        if step == 0:
            acc[...] = source[pl.ds(keep, size)].astype(F32) + arrived
        else:
            spot = pl.ds(start_of(order, step) + keep, size)
            acc[spot] = acc[spot] + arrived

    for index in range(3):
        send(index, 0)
    for step in range(steps):
        for index in range(3):
            add(index, step)
            if step + 1 < steps:
                send(index, step + 1)
    for step in range(steps):
        for index in range(3):
            copies[index, step].wait_send()

    lines = k_ref.shape[1] // 2
    half = k_ref.shape[2]
    model = 2 * half
    head = model // HEADS
    k_sum = k_acc[pl.ds(start_of(orders[0], steps), 1)][0]
    q_sum = q_acc[pl.ds(start_of(orders[1], steps), 1)][0]
    s_sum = s_acc[pl.ds(start_of(orders[0], steps), 1)][0]
    logit_ref[...] = s_sum[:8]
    lane_head = lax.broadcasted_iota(jnp.int32, (128, model), 1) // head
    open_up = lax.broadcasted_iota(jnp.int32, (128, model), 0) == lane_head
    open_up = jnp.where(open_up, 1.0, 0.0).astype(BF)
    value = jnp.zeros((lines, model), F32)
    rest = s_sum
    for step in range(3):
        piece = rest.astype(BF)
        rest = rest - piece.astype(F32)
        value = value + nn(piece, open_up)
    value = value * mh_ref[...]
    gq_ref[:, :half] = q_sum[:rows]
    gq_ref[:, half:] = q_sum[lines:lines + rows]
    gkv_ref[:, :half] = k_sum[:rows]
    gkv_ref[:, half:model] = k_sum[lines:lines + rows]
    gkv_ref[:, model:] = value[:rows]


def bit_orders(groups, devices):
    low = devices.bit_length() - 1
    across = list(range(low, low + groups.bit_length() - 1))
    along = list(range(1, low))
    return (0, *across, *along), (0, *reversed(across), *along)


def places(total, order):
    at = np.arange(total)
    owner = np.zeros(total, np.int32)
    for step, bit in enumerate(order):
        owner |= ((at >> (len(order) - 1 - step)) & 1) << bit
    return owner


def feature_rows(model, total, order):
    rows = model // total
    lines = up(rows, 8)
    line = np.arange(lines)[None, :]
    feat = np.where(line < rows, places(total, order)[:, None] * rows + line, -1)
    return feat.reshape(-1, 1).astype(np.int32)


def local(image_tokens, text_tokens, negatives, query_weight, kv_weight, match_head, cotangent):
    count, length, model = image_tokens.shape
    text_len = text_tokens.shape[1]
    devices = lax.axis_size("dev")
    groups = lax.axis_size("grp")
    capacity = max(2, (2 * count + devices - 1) // devices)
    padded = up(length, 256)
    texts = devices * count
    slots = count + devices * capacity

    owner = negatives // count
    meta = jnp.concatenate(
        [cotangent, owner.astype(BF), (negatives - owner * count).astype(BF)], axis=1
    )
    meta = jnp.pad(meta, ((0, 0), (0, model - meta.shape[1])))[:, None, :]
    message = jnp.concatenate(
        [text_tokens, meta, jnp.zeros((count, ROWS - text_len - 1, model), BF)], axis=1
    )
    everyone = lax.all_gather(message, "dev", axis=0, tiled=True)

    keys, gains, pictures = pl.pallas_call(
        keys_kernel,
        out_shape=(
            jax.ShapeDtypeStruct((count, padded, model), BF),
            jax.ShapeDtypeStruct((count, 16, padded), F32),
            jax.ShapeDtypeStruct((count, padded, model), BF),
        ),
        in_specs=[VMEM] * 3,
        out_specs=(VMEM,) * 3,
        compiler_params=pltpu.CompilerParams(vmem_limit_bytes=BIG),
        cost_estimate=pl.CostEstimate(
            flops=4 * count * padded * model * model, bytes_accessed=8 * 1024 * 1024,
            transcendentals=0,
        ),
    )(image_tokens, kv_weight, match_head.reshape(1, model))

    facts = everyone[:, text_len, :8].astype(F32)
    owners = facts[:, 3:5].astype(jnp.int32).reshape(-1)
    locals_ = facts[:, 5:7].astype(jnp.int32).reshape(-1)
    tangents = facts[:, :3].reshape(-1)
    total = groups * devices
    rows = model // total
    lines = up(rows, 8)
    half = model // 2
    orders = bit_orders(groups, devices)
    feat_k, feat_q = (feature_rows(model, total, order) for order in orders)
    home = np.argsort(places(total, orders[0])).astype(np.int32) * lines
    home = np.repeat(home, count * 3).reshape(groups, 1, texts * 3)
    home = lax.dynamic_index_in_dim(jnp.asarray(home), lax.axis_index("grp"), 0, keepdims=False)
    grad_k, grad_q, small = pl.pallas_call(
        functools.partial(pairs_kernel, length, text_len),
        out_shape=(
            jax.ShapeDtypeStruct((total, 2 * lines, half), BF),
            jax.ShapeDtypeStruct((total, 2 * lines, half), BF),
            jax.ShapeDtypeStruct((total, lines, 128), F32),
        ),
        in_specs=[SMEM] * 3 + [VMEM] * 8,
        out_specs=(VMEM,) * 3,
        scratch_shapes=[
            pltpu.VMEM((slots * ROWS, model), BF),
            pltpu.VMEM((slots * ROWS, model), BF),
            pltpu.VMEM((count, padded, model), F32),
            pltpu.VMEM((slots * ROWS, model), BF),
            pltpu.VMEM((count, 128, padded), F32),
            pltpu.VMEM((texts * 3, padded), F32),
            pltpu.SMEM((slots,), jnp.int32),
            pltpu.SMEM((slots,), jnp.int32),
            pltpu.SMEM((slots,), jnp.int32),
        ],
        compiler_params=pltpu.CompilerParams(vmem_limit_bytes=BIG),
        cost_estimate=pl.CostEstimate(
            flops=20 * 1024**3, bytes_accessed=16 * 1024 * 1024, transcendentals=0
        ),
    )(owners, locals_, tangents, feat_k, feat_q, home, pictures, keys, gains, everyone,
      query_weight)

    steps = len(orders[0])
    grad_query, grad_kv, answers = pl.pallas_call(
        functools.partial(reduce_kernel, rows, orders),
        out_shape=(
            jax.ShapeDtypeStruct((rows, model), F32),
            jax.ShapeDtypeStruct((rows, 2 * model), F32),
            jax.ShapeDtypeStruct((8, 128), F32),
        ),
        in_specs=[VMEM] * 4,
        out_specs=(VMEM,) * 3,
        scratch_shapes=[
            pltpu.VMEM((total // 2, 2 * lines, half), F32),
            pltpu.VMEM((total // 2, 2 * lines, half), F32),
            pltpu.VMEM((total // 2, lines, 128), F32),
            pltpu.VMEM((total // 2, 2 * lines, half), BF),
            pltpu.VMEM((total // 2, 2 * lines, half), BF),
            pltpu.VMEM((total // 2, lines, 128), F32),
            pltpu.VMEM((total, 2 * lines, half), BF),
            pltpu.VMEM((total, 2 * lines, half), BF),
            pltpu.VMEM((total, lines, 128), F32),
            pltpu.SemaphoreType.DMA((3, steps)),
            pltpu.SemaphoreType.DMA((3, steps)),
        ],
        compiler_params=pltpu.CompilerParams(
            vmem_limit_bytes=40 * 1024 * 1024, collective_id=0, has_side_effects=True
        ),
        cost_estimate=pl.CostEstimate(
            flops=1024**2, bytes_accessed=8 * 1024 * 1024, transcendentals=0
        ),
    )(grad_k, grad_q, small, match_head.reshape(1, model))
    logits = answers[0, 16:16 + 3 * count].reshape(count, 3)
    return (logits, grad_query, grad_kv)


def solution(mesh):
    placed = (
        P(("grp", "dev"), None, None),
        P(("grp", "dev"), None, None),
        P(("grp", "dev"), None),
        P(),
        P(),
        P(),
        P(("grp", "dev"), None),
    )
    return jax.shard_map(
        local,
        mesh=mesh,
        in_specs=placed,
        out_specs=(P(("grp", "dev"), None), P(("grp", "dev"), None), P(("grp", "dev"), None)),
        check_vma=False,
    )
```

```python
import functools

import jax
import jax.numpy as jnp
import numpy as np
from jax import lax
from jax.experimental import pallas as pl
from jax.experimental.pallas import tpu as pltpu
from jax.sharding import PartitionSpec as P

HEADS = 12
PACK = 4
ROWS = 32
BF = jnp.bfloat16
F32 = jnp.float32
VMEM = pl.BlockSpec(memory_space=pltpu.VMEM)
SMEM = pl.BlockSpec(memory_space=pltpu.SMEM)
BIG = 56 * 1024 * 1024


def up(value, unit):
    return (value + unit - 1) // unit * unit


def nt(left, right):
    return lax.dot_general(left, right, (((1,), (1,)), ((), ())), preferred_element_type=F32)


def tn(left, right):
    return lax.dot_general(left, right, (((0,), (0,)), ((), ())), preferred_element_type=F32)


def nn(left, right):
    return jnp.dot(left, right, preferred_element_type=F32)


def one_hot(feat, model):
    lanes = lax.broadcasted_iota(jnp.int32, (feat.shape[0], model), 1)
    return jnp.where(lanes == feat, 1.0, 0.0).astype(BF)


def keys_kernel(x_ref, w_ref, mh_ref, feat_ref, k_ref, u_ref, flip_ref, xp_ref):
    count, length, model = x_ref.shape
    head = model // HEADS
    gain = mh_ref[...]
    high = gain.astype(BF).astype(F32)
    middle = (gain - high).astype(BF).astype(F32)
    low = gain - high - middle
    rows = lax.broadcasted_iota(jnp.int32, (16, model), 0)
    lanes = lax.broadcasted_iota(jnp.int32, (16, model), 1)
    inside = (lanes >= rows * head) & (lanes < rows * head + head)
    parts = [jnp.where(inside, part, 0.0).astype(BF) for part in (high, middle, low)]
    turn = one_hot(feat_ref[...], model)
    for image in range(count):
        xp_ref[image] = jnp.zeros(xp_ref.shape[1:], BF)
        xp_ref[image, :length, :] = x_ref[image]
        rows_in = xp_ref[image]
        padded = rows_in.shape[0]
        flip_ref[:, image * padded:(image + 1) * padded] = nt(turn, rows_in).astype(BF)
        k_ref[image] = nn(rows_in, w_ref[:, :model]).astype(BF)
        values = nn(rows_in, w_ref[:, model:]).astype(BF)
        u_ref[image] = nt(parts[0], values) + nt(parts[1], values) + nt(parts[2], values)


def pairs_kernel(
    length, text_len, owner_ref, local_ref, tangent_ref, feat_q_ref, home_ref, flip_ref,
    k_ref, u_ref, t_ref, wq_ref, gk_ref, gq_ref, small_ref,
    tp_ref, q_ref, dk_ref, dq_ref, s_ref, lg_ref, text_s, col_s, image_s,
):
    count, padded, model = k_ref.shape
    head = model // HEADS
    width = PACK * head
    block = PACK * ROWS
    factor = head ** (-0.5)
    me = lax.axis_index("dev")
    requests = owner_ref.shape[0]
    outs = tangent_ref.shape[0]
    for slot in range(text_s.shape[0]):
        text_s[slot] = 0
        col_s[slot] = 0
        image_s[slot] = 0
    real = lax.broadcasted_iota(jnp.int32, (ROWS, model), 0) < text_len

    def place(slot, text):
        rows = jnp.where(real, t_ref[text].astype(F32), 0.0).astype(BF)
        tp_ref[pl.ds(pl.multiple_of(slot * ROWS, ROWS), ROWS), :] = rows

    tp_ref[...] = jnp.zeros(tp_ref.shape, BF)
    dq_ref[...] = jnp.zeros(dq_ref.shape, BF)
    dk_ref[...] = jnp.zeros(dk_ref.shape, F32)
    s_ref[...] = jnp.zeros(s_ref.shape, F32)
    lg_ref[...] = jnp.zeros(lg_ref.shape, F32)
    for image in range(count):
        text_s[image] = me * count + image
        col_s[image] = 0
        image_s[image] = image
        place(image, me * count + image)

    def look(request, filled):
        mine = owner_ref[request] == me

        @pl.when(mine)
        def _():
            text = request // 2
            text_s[filled] = text
            col_s[filled] = request - 2 * text + 1
            image_s[filled] = local_ref[request]
            place(filled, text)

        return filled + mine.astype(jnp.int32)

    used = lax.fori_loop(0, requests, look, jnp.int32(count))
    q_ref[...] = nn(tp_ref[...], wq_ref[...]).astype(BF)

    row_head = lax.broadcasted_iota(jnp.int32, (block, width), 0) // ROWS
    lane_head = lax.broadcasted_iota(jnp.int32, (block, width), 1) // head
    diagonal = row_head == lane_head
    short_head = lax.broadcasted_iota(jnp.int32, (ROWS, width), 1) // head
    beyond = lax.broadcasted_iota(jnp.int32, (block, padded), 1) >= length
    sum_row = lax.broadcasted_iota(jnp.int32, (16, block), 0)
    sum_lane = lax.broadcasted_iota(jnp.int32, (16, block), 1)
    counted = (sum_lane // ROWS == sum_row) & (sum_lane % ROWS < text_len)
    summer = jnp.where(counted, 1.0, 0.0).astype(BF)

    together = 2

    def pairs(turn, carry):
        slots = [turn * together + extra for extra in range(together)]
        images = [image_s[slot] for slot in slots]
        wheres = [text_s[slot] * 3 + col_s[slot] for slot in slots]
        scales = [
            jnp.where(slot < used, tangent_ref[where], 0.0) / text_len
            for slot, where in zip(slots, wheres)
        ]
        rows = [pl.ds(pl.multiple_of(slot * ROWS, ROWS), ROWS) for slot in slots]
        jobs = [(each, pack) for each in range(together) for pack in range(HEADS // PACK)]
        cols = [slice(pack * width, (pack + 1) * width) for _, pack in jobs]
        spreads, keys, probs, weights, gains, lows = [], [], [], [], [], []
        for job, (each, pack) in enumerate(jobs):
            four = q_ref[rows[each], cols[job]].astype(F32)
            tall = jnp.concatenate([four] * PACK, axis=0)
            spreads.append(jnp.where(diagonal, tall, 0.0).astype(BF))
            keys.append(k_ref[images[each], :, cols[job]])
            gains.append(u_ref[images[each], pack * PACK:(pack + 1) * PACK, :])
        scores = [nt(spread, key) for spread, key in zip(spreads, keys)]
        for score in scores:
            score = jnp.where(beyond, -1e30, score * factor)
            score = jnp.exp(score - jnp.max(score, axis=1, keepdims=True))
            probs.append(score * (1.0 / jnp.sum(score, axis=1, keepdims=True)))
        for job, (each, pack) in enumerate(jobs):
            weights.append(nn(summer, probs[job].astype(BF))[:PACK])
            d_probs = jnp.concatenate(
                [
                    jnp.broadcast_to(gains[job][h:h + 1] * scales[each], (ROWS, padded))
                    for h in range(PACK)
                ],
                axis=0,
            )
            centre = jnp.sum(probs[job] * d_probs, axis=1, keepdims=True)
            lows.append((probs[job] * (d_probs - centre)).astype(BF))
        d_keys = [tn(low, spread) for low, spread in zip(lows, spreads)]
        wides = [nn(low, key) for low, key in zip(lows, keys)]
        for job, (each, pack) in enumerate(jobs):
            kept = jnp.zeros((ROWS, width), F32)
            for h in range(PACK):
                kept = jnp.where(short_head == h, wides[job][h * ROWS:(h + 1) * ROWS], kept)
            dq_ref[rows[each], cols[job]] = (kept * factor).astype(BF)
            heads = slice(pack * PACK, (pack + 1) * PACK)
            s_ref[images[each], heads, :] += weights[job] * scales[each]
            dk_ref[images[each], :, cols[job]] += d_keys[job]
        for each in reversed(range(together)):
            total = jnp.zeros((1, padded), F32)
            for job, (owner, pack) in enumerate(jobs):
                if owner == each:
                    total = total + jnp.sum(weights[job] * gains[job], axis=0, keepdims=True)
            live = slots[each] < used
            spot = pl.ds(jnp.where(live, wheres[each], outs), 1)
            lg_ref[spot, :] = total * (1.0 / text_len)
        return carry

    lax.fori_loop(0, (used + together - 1) // together, pairs, 0)

    blocks, tall_rows, half = gq_ref.shape
    lines = tall_rows // 2

    def store(out_ref, left, right):
        sides = [
            nn(left, right[:, side * half:(side + 1) * half]).reshape(blocks, lines, half)
            for side in range(2)
        ]
        out_ref[...] = jnp.concatenate(sides, axis=1).astype(BF)

    turn_q = one_hot(feat_q_ref[...], model)
    store(gq_ref, nt(turn_q, tp_ref[...]).astype(BF), dq_ref[...])
    flipped = flip_ref[...]
    store(gk_ref, flipped, (dk_ref[...] * factor).astype(BF).reshape(count * padded, model))

    answers = jnp.sum(lg_ref[:outs], axis=1, keepdims=True)
    lane = lax.broadcasted_iota(jnp.int32, (outs, 128), 1)
    line = lax.broadcasted_iota(jnp.int32, (outs, 128), 0)
    rest = jnp.where(lane - 16 == line % (3 * count), answers, 0.0)
    homes = lax.broadcasted_iota(jnp.int32, (blocks * lines, outs), 0) == home_ref[...]
    homes = jnp.where(homes, 1.0, 0.0).astype(BF)
    small = jnp.zeros((blocks * lines, 128), F32)
    for step in range(3):
        piece = rest.astype(BF)
        rest = rest - piece.astype(F32)
        small = small + nn(homes, piece)
    for image in range(count):
        weights = s_ref[image]
        high = weights.astype(BF)
        low = (weights - high.astype(F32)).astype(BF)
        mine = flipped[:, image * padded:(image + 1) * padded]
        small = small + nt(mine, high) + nt(mine, low)
    small_ref[...] = small.reshape(blocks, lines, 128)


def reduce_kernel(
    rows, orders, k_ref, q_ref, small_ref, mh_ref, gq_ref, gkv_ref, logit_ref,
    k_acc, q_acc, s_acc, k_send, q_send, s_send, k_recv, q_recv, s_recv, send_sem, recv_sem,
):
    devices = lax.axis_size("dev")
    me = lax.axis_index("grp") * devices + lax.axis_index("dev")
    blocks = k_ref.shape[0]
    steps = len(orders[0])

    def bit_of(bit):
        return lax.rem(lax.div(me, 1 << bit), 2)

    def partner(bit):
        other = me + (1 - 2 * bit_of(bit)) * (1 << bit)
        return (lax.div(other, devices), lax.rem(other, devices))

    barrier = pltpu.get_barrier_semaphore()
    for bit in range(steps):
        pl.semaphore_signal(
            barrier, inc=1, device_id=partner(bit), device_id_type=pl.DeviceIdType.MESH
        )
    pl.semaphore_wait(barrier, steps)

    streams = (
        (k_ref, k_acc, k_send, k_recv, orders[0]),
        (q_ref, q_acc, q_send, q_recv, orders[1]),
        (small_ref, s_acc, s_send, s_recv, orders[0]),
    )
    copies = {}

    def send(index, step):
        source, acc, staged, landed, order = streams[index]
        size = blocks >> (step + 1)
        base = blocks - 2 * size
        away = (1 - bit_of(order[step])) * size
        if step == 0:
            held = source.at[pl.ds(away, size)]
        else:
            lower = base - blocks // 2
            held = staged.at[pl.ds(lower, size)]
            staged[pl.ds(lower, size)] = acc[pl.ds(start_of(order, step) + away, size)].astype(
                staged.dtype
            )
        copies[index, step] = pltpu.make_async_remote_copy(
            src_ref=held,
            dst_ref=landed.at[pl.ds(base, size)],
            send_sem=send_sem.at[index, step],
            recv_sem=recv_sem.at[index, step],
            device_id=partner(order[step]),
            device_id_type=pl.DeviceIdType.MESH,
        )
        copies[index, step].start()

    def start_of(order, step):
        start = 0
        for earlier in range(1, step):
            start = start + bit_of(order[earlier]) * (blocks >> (earlier + 1))
        return start

    def add(index, step):
        source, acc, staged, landed, order = streams[index]
        size = blocks >> (step + 1)
        base = blocks - 2 * size
        copies[index, step].wait_recv()
        arrived = landed[pl.ds(base, size)].astype(F32)
        keep = bit_of(order[step]) * size
        if step == 0:
            acc[...] = source[pl.ds(keep, size)].astype(F32) + arrived
        else:
            spot = pl.ds(start_of(order, step) + keep, size)
            acc[spot] = acc[spot] + arrived

    for index in range(3):
        send(index, 0)
    for step in range(steps):
        for index in range(3):
            add(index, step)
            if step + 1 < steps:
                send(index, step + 1)
    for step in range(steps):
        for index in range(3):
            copies[index, step].wait_send()

    lines = k_ref.shape[1] // 2
    half = k_ref.shape[2]
    model = 2 * half
    head = model // HEADS
    k_sum = k_acc[pl.ds(start_of(orders[0], steps), 1)][0]
    q_sum = q_acc[pl.ds(start_of(orders[1], steps), 1)][0]
    s_sum = s_acc[pl.ds(start_of(orders[0], steps), 1)][0]
    logit_ref[...] = s_sum[:8]
    lane_head = lax.broadcasted_iota(jnp.int32, (128, model), 1) // head
    open_up = lax.broadcasted_iota(jnp.int32, (128, model), 0) == lane_head
    open_up = jnp.where(open_up, 1.0, 0.0).astype(BF)
    value = jnp.zeros((lines, model), F32)
    rest = s_sum
    for step in range(3):
        piece = rest.astype(BF)
        rest = rest - piece.astype(F32)
        value = value + nn(piece, open_up)
    value = value * mh_ref[...]
    gq_ref[:, :half] = q_sum[:rows]
    gq_ref[:, half:] = q_sum[lines:lines + rows]
    gkv_ref[:, :half] = k_sum[:rows]
    gkv_ref[:, half:model] = k_sum[lines:lines + rows]
    gkv_ref[:, model:] = value[:rows]


def bit_orders(groups, devices):
    low = devices.bit_length() - 1
    across = list(range(low, low + groups.bit_length() - 1))
    along = list(range(1, low))
    return (0, *across, *along), (0, *reversed(across), *along)


def places(total, order):
    at = np.arange(total)
    owner = np.zeros(total, np.int32)
    for step, bit in enumerate(order):
        owner |= ((at >> (len(order) - 1 - step)) & 1) << bit
    return owner


def feature_rows(model, total, order):
    rows = model // total
    lines = up(rows, 8)
    line = np.arange(lines)[None, :]
    feat = np.where(line < rows, places(total, order)[:, None] * rows + line, -1)
    return feat.reshape(-1, 1).astype(np.int32)


def local(image_tokens, text_tokens, negatives, query_weight, kv_weight, match_head, cotangent):
    count, length, model = image_tokens.shape
    text_len = text_tokens.shape[1]
    devices = lax.axis_size("dev")
    groups = lax.axis_size("grp")
    capacity = max(2, (2 * count + devices - 1) // devices)
    padded = up(length, 256)
    texts = devices * count
    slots = up(count + devices * capacity, 2)

    owner = negatives // count
    meta = jnp.concatenate(
        [cotangent, owner.astype(BF), (negatives - owner * count).astype(BF)], axis=1
    )
    meta = jnp.pad(meta, ((0, 0), (0, model - meta.shape[1])))[:, None, :]
    message = jnp.concatenate(
        [text_tokens, meta, jnp.zeros((count, ROWS - text_len - 1, model), BF)], axis=1
    )
    everyone = lax.all_gather(message, "dev", axis=0, tiled=True)

    total = groups * devices
    rows = model // total
    lines = up(rows, 8)
    half = model // 2
    orders = bit_orders(groups, devices)
    feat_k, feat_q = (feature_rows(model, total, order) for order in orders)
    keys, gains, flipped = pl.pallas_call(
        keys_kernel,
        out_shape=(
            jax.ShapeDtypeStruct((count, padded, model), BF),
            jax.ShapeDtypeStruct((count, 16, padded), F32),
            jax.ShapeDtypeStruct((total * lines, count * padded), BF),
        ),
        in_specs=[VMEM] * 4,
        out_specs=(VMEM,) * 3,
        scratch_shapes=[pltpu.VMEM((count, padded, model), BF)],
        compiler_params=pltpu.CompilerParams(vmem_limit_bytes=BIG),
        cost_estimate=pl.CostEstimate(
            flops=4 * count * padded * model * model, bytes_accessed=8 * 1024 * 1024,
            transcendentals=0,
        ),
    )(image_tokens, kv_weight, match_head.reshape(1, model), feat_k)

    facts = everyone[:, text_len, :8].astype(F32)
    owners = facts[:, 3:5].astype(jnp.int32).reshape(-1)
    locals_ = facts[:, 5:7].astype(jnp.int32).reshape(-1)
    tangents = facts[:, :3].reshape(-1)
    home = np.argsort(places(total, orders[0])).astype(np.int32) * lines
    home = np.repeat(home, count * 3).reshape(groups, 1, texts * 3)
    home = lax.dynamic_index_in_dim(jnp.asarray(home), lax.axis_index("grp"), 0, keepdims=False)
    grad_k, grad_q, small = pl.pallas_call(
        functools.partial(pairs_kernel, length, text_len),
        out_shape=(
            jax.ShapeDtypeStruct((total, 2 * lines, half), BF),
            jax.ShapeDtypeStruct((total, 2 * lines, half), BF),
            jax.ShapeDtypeStruct((total, lines, 128), F32),
        ),
        in_specs=[SMEM] * 3 + [VMEM] * 7,
        out_specs=(VMEM,) * 3,
        scratch_shapes=[
            pltpu.VMEM((slots * ROWS, model), BF),
            pltpu.VMEM((slots * ROWS, model), BF),
            pltpu.VMEM((count, padded, model), F32),
            pltpu.VMEM((slots * ROWS, model), BF),
            pltpu.VMEM((count, 128, padded), F32),
            pltpu.VMEM((texts * 3 + 8, padded), F32),
            pltpu.SMEM((slots,), jnp.int32),
            pltpu.SMEM((slots,), jnp.int32),
            pltpu.SMEM((slots,), jnp.int32),
        ],
        compiler_params=pltpu.CompilerParams(vmem_limit_bytes=BIG),
        cost_estimate=pl.CostEstimate(
            flops=20 * 1024**3, bytes_accessed=16 * 1024 * 1024, transcendentals=0
        ),
    )(owners, locals_, tangents, feat_q, home, flipped, keys, gains, everyone,
      query_weight)

    steps = len(orders[0])
    grad_query, grad_kv, answers = pl.pallas_call(
        functools.partial(reduce_kernel, rows, orders),
        out_shape=(
            jax.ShapeDtypeStruct((rows, model), F32),
            jax.ShapeDtypeStruct((rows, 2 * model), F32),
            jax.ShapeDtypeStruct((8, 128), F32),
        ),
        in_specs=[VMEM] * 4,
        out_specs=(VMEM,) * 3,
        scratch_shapes=[
            pltpu.VMEM((total // 2, 2 * lines, half), F32),
            pltpu.VMEM((total // 2, 2 * lines, half), F32),
            pltpu.VMEM((total // 2, lines, 128), F32),
            pltpu.VMEM((total // 2, 2 * lines, half), BF),
            pltpu.VMEM((total // 2, 2 * lines, half), BF),
            pltpu.VMEM((total // 2, lines, 128), F32),
            pltpu.VMEM((total, 2 * lines, half), BF),
            pltpu.VMEM((total, 2 * lines, half), BF),
            pltpu.VMEM((total, lines, 128), F32),
            pltpu.SemaphoreType.DMA((3, steps)),
            pltpu.SemaphoreType.DMA((3, steps)),
        ],
        compiler_params=pltpu.CompilerParams(
            vmem_limit_bytes=40 * 1024 * 1024, collective_id=0, has_side_effects=True
        ),
        cost_estimate=pl.CostEstimate(
            flops=1024**2, bytes_accessed=8 * 1024 * 1024, transcendentals=0
        ),
    )(grad_k, grad_q, small, match_head.reshape(1, model))
    logits = answers[0, 16:16 + 3 * count].reshape(count, 3)
    return (logits, grad_query, grad_kv)


def solution(mesh):
    placed = (
        P(("grp", "dev"), None, None),
        P(("grp", "dev"), None, None),
        P(("grp", "dev"), None),
        P(),
        P(),
        P(),
        P(("grp", "dev"), None),
    )
    return jax.shard_map(
        local,
        mesh=mesh,
        in_specs=placed,
        out_specs=(P(("grp", "dev"), None), P(("grp", "dev"), None), P(("grp", "dev"), None)),
        check_vma=False,
    )
```
